32 devices in a mesh: slab: 8 (over z, core), quad: 4 (over y, x).
Axes of the slice: x: 2, y: 2, z: 4, core: 2. Of those that a mesh axis runs over, the one named last changes fastest.
Arguments:
- absorption: bfloat16 [4, 1048576], P(None, ('slab', 'quad')), may hold values from 0.19921875 to 5
- emission: float32 [8, 128, 1024], P('slab'), may hold values from 1 to 4
- weights: float32 [4], P('quad'), may hold values from 0.01 to 0.06
- low_bound: float32 [4], P('quad'), may hold values from 0.1 to 1
- high_bound: float32 [4], P('quad'), may hold values from 12.5 to 16
- row_counts: int32 [8, 4], P('slab'), may hold values from 1 to 512, 1024 in all within a row
Outputs:
- source_rows: float32 [16384, 128], P(('slab', 'quad'))
The draws below stay inside these ranges and needn't reach their ends.
Inputs may be any that keep to these rules, and one draw needn't show every extreme that they name: `row_counts`: each row of 4 counts sums to 1024, and its largest is exactly 512.
All inputs are finite; a program needn't handle non-finite values.
Results may differ from the reference program's by a relative error of at most 0.0015.
Values may be sent and summed in bfloat16 or wider, within the bound.
No kernel may reach another device: no remote copies, remote signals or barrier semaphores. Data moves between devices by JAX's collectives and lax.ppermute only.
A program may use at most 64 MiB of HBM per device.

```python
import math
import jax
import jax.numpy as jnp
import numpy as np
from jax import lax

NY = 128
NZ = 1024
ITERS = 3
G = 4
NX = 8
CELLS = 1048576
ROWS_SLAB = 1024
MOST = 512
N_SLAB = 8
N_QUAD = 4


def levels(rng, dims, shards, low, top_value):
    def one(axis_at, parts):
        heights = jax.random.uniform(jax.random.fold_in(jax.random.fold_in(rng, 6), axis_at), (parts,), jnp.float32, low / len(shards), top_value / len(shards))
        return jnp.repeat(jnp.exp(heights), dims[axis_at] // parts).reshape((-1,) + (1,) * (len(dims) - axis_at - 1))

    loudness = one(*shards[0])
    for cut in shards[1:]:
        loudness = loudness * one(*cut)
    return loudness


def profile(number_of, total, reach, lean):
    weights = [(1 << 20) // math.isqrt(grade ** lean) + 1 for grade in range(2, number_of + 1)]
    surplus, given = total - reach - (number_of - 1), [1] * (number_of - 1)
    while surplus > 0:
        candidates = [i for i in range(number_of - 1) if given[i] < reach]
        whole, budget = sum([weights[i] for i in candidates]), surplus
        for i in candidates:
            extra = min(reach - given[i], max(1, budget * weights[i] // whole), surplus)
            given[i] = given[i] + extra
            surplus = surplus - extra
    return np.array([reach] + given)


def uneven_parts(key, number_of, total, most, lean):
    if number_of == 2:
        one = jax.random.randint(key, (), max(1, total - most), min(most, total - 1) + 1)
        return jnp.stack([one, total - one])
    lengths = jnp.asarray(profile(number_of, total, most, lean), jnp.int32)
    pairs = (number_of - 1) // 2
    donor, receiver = lengths[1:1 + 2 * pairs:2], lengths[2:2 + 2 * pairs:2]
    room = jnp.minimum(donor - 1, most - receiver)
    moved = jax.random.randint(jax.random.fold_in(key, 1), (pairs,), 0, 1 << 20) % (room + 1)
    lengths = lengths.at[1:1 + 2 * pairs:2].set(donor - moved).at[2:2 + 2 * pairs:2].set(receiver + moved)
    return lengths[jax.random.permutation(jax.random.fold_in(key, 2), number_of)]


def setup_inputs(seed: int = 0) -> dict:
    keys = jax.random.split(jax.random.key(seed), 7)
    return {
        "absorption": jnp.clip(jnp.exp(math.log(5.0) - 3.2227897 * jax.random.uniform(keys[0], (G, CELLS), jnp.float32) ** levels(keys[0], (G, CELLS), ((1, 32),), -0.2, 0.2)), 0.19921875, 5.0).astype(jnp.bfloat16),
        "emission": jnp.clip(jnp.exp(math.log(4.0) - 1.3862944 * jax.random.uniform(keys[1], (NX, NY, NZ), jnp.float32) ** levels(keys[1], (NX, NY, NZ), ((0, 8),), -0.2, 0.2)), 1.0, 4.0),
        "weights": jnp.clip(jnp.exp(math.log(0.06) - 1.7917595 * jax.random.uniform(keys[2], (G,), jnp.float32) ** levels(keys[2], (G,), ((0, 4),), -0.2, 0.2)), 0.01, 0.06),
        "low_bound": jnp.clip(0.1 + 0.9 * jax.random.uniform(keys[3], (G,), jnp.float32) ** levels(keys[3], (G,), ((0, 4),), -0.2, 0.2), 0.1, 1.0),
        "high_bound": jnp.clip(12.5 + 3.5 * jax.random.uniform(keys[4], (G,), jnp.float32) ** levels(keys[4], (G,), ((0, 4),), -0.2, 0.2), 12.5, 16.0),
        "row_counts": jax.vmap(lambda own: uneven_parts(own, N_QUAD, ROWS_SLAB, MOST, 2))(jax.random.split(keys[5], N_SLAB)).reshape((N_SLAB, N_QUAD)).astype(jnp.int32),
    }


def operate(fields, kappa_grid):
    padded = jnp.pad(fields, ((0, 0), (1, 1), (1, 1), (1, 1)))
    center_cells = padded[:, 1:-1, 1:-1, 1:-1]
    neighbours = padded[:, 2:, 1:-1, 1:-1] + padded[:, :-2, 1:-1, 1:-1]
    neighbours = neighbours + padded[:, 1:-1, 2:, 1:-1] + padded[:, 1:-1, :-2, 1:-1]
    neighbours = neighbours + padded[:, 1:-1, 1:-1, 2:] + padded[:, 1:-1, 1:-1, :-2]
    laplace_term = 6.0 * center_cells - neighbours
    first_out = kappa_grid * (fields[0] - (2.0 / 3.0) * fields[1]) + laplace_term[0] / 3.0
    second_out = kappa_grid * (fields[1] - (2.0 / 3.0) * fields[0]) + laplace_term[1] / 7.0
    return jnp.stack([first_out, second_out])


def reference(absorption, emission, weights, low_bound, high_bound, row_counts):
    grid_kappa = absorption.reshape(G, NX, NY, NZ)

    def one_point(total, items):
        kappa_half, weight, low, high = items
        kappa_grid = kappa_half.astype(jnp.float32)
        source = weight * kappa_grid * emission
        rhs_pair = jnp.stack([source, (-2.0 / 3.0) * source])
        mid_bound = (high + low) / 2.0
        half_width = (high - low) / 2.0
        sigma_pt = mid_bound / half_width
        rho_now = 1.0 / sigma_pt
        solution = jnp.zeros_like(rhs_pair)
        resid = rhs_pair
        direction = rhs_pair / mid_bound
        for sweep_no in range(ITERS):
            solution = solution + direction
            if sweep_no + 1 < ITERS:
                image = operate(direction, kappa_grid)
                resid = resid - image
                rho_next = 1.0 / (2.0 * sigma_pt - rho_now)
                direction = rho_next * rho_now * direction + (2.0 * rho_next / half_width) * resid
                rho_now = rho_next
        incident = solution[0] - (2.0 / 3.0) * solution[1]
        return total + kappa_grid * (incident - weight * emission), None

    start_total = jnp.zeros((NX, NY, NZ), jnp.float32)
    total, unused = lax.scan(one_point, start_total, (grid_kappa, weights, low_bound, high_bound))
    slab_rows = total.reshape(N_SLAB, ROWS_SLAB, 128)
    padded_rows = jnp.concatenate([slab_rows, jnp.zeros((N_SLAB, MOST, 128), jnp.float32)], axis=1)
    offsets = (jnp.cumsum(row_counts, axis=1) - row_counts).astype(jnp.int32)
    row_index = offsets[:, :, None] + jnp.arange(MOST, dtype=jnp.int32)[None, None, :]
    slab_index = jnp.arange(N_SLAB, dtype=jnp.int32)[:, None, None]
    picked = padded_rows[slab_index, row_index]
    keep_rows = jnp.arange(MOST, dtype=jnp.int32)[None, None, :] < row_counts[:, :, None]
    picked = jnp.where(keep_rows[:, :, :, None], picked, jnp.zeros_like(picked))
    return picked.reshape(N_SLAB * N_QUAD * MOST, 128)
```

```python
import functools

import jax
import jax.numpy as jnp
from jax import lax
from jax.experimental import pallas as pl
from jax.experimental.pallas import tpu as pltpu
from jax.sharding import PartitionSpec as P

LANES = 128
F32 = jnp.float32
BF16 = jnp.bfloat16
ANY = pl.BlockSpec(memory_space=pl.ANY)
SMEM = pl.BlockSpec(memory_space=pltpu.SMEM)
VMEM = pl.BlockSpec(memory_space=pltpu.VMEM)


class Sizes:
    def __init__(self, absorption, emission, n_slab, n_quad):
        self.points = absorption.shape[0]
        self.ny, self.nz = emission.shape[1:]
        self.chunks = self.nz // LANES
        self.rows_quad = absorption.shape[1] // self.nz
        self.rows = self.rows_quad // 2
        self.ext = self.rows + 4
        self.per_row = self.points * self.chunks
        self.e_rows = min(self.ny, (6 + self.ext + 7) // 8 * 8)
        self.n_slab, self.n_quad = n_slab, n_quad
        self.field = self.rows * self.per_row
        self.plain = self.rows * self.chunks


def place():
    slab = lax.axis_index("slab")
    return lax.div(slab, 2), lax.rem(slab, 2), lax.axis_index("quad")


def load_planes(sz, k_own, k_pair, halo_own, halo_pair, e_own, e_pair, k_raw, e_raw, sems):
    _, core, quad = place()
    first = quad * sz.rows_quad + core * sz.rows - 2
    start = jnp.clip(lax.div(first + 8, 8) * 8 - 8, 0, sz.ny - sz.e_rows)
    start = pl.multiple_of(start, 8)
    other = 1 - core
    inner = (sz.rows + 2) * sz.per_row
    outer = 2 * sz.per_row
    copies = []
    for plane, ref, halo in ((core, k_own, halo_own), (other, k_pair, halo_pair)):
        src = pl.multiple_of(core * ((sz.rows - 2) * sz.per_row), 16)
        dst = pl.multiple_of(other * outer, 16)
        copies.append((ref.at[pl.ds(src, inner)], k_raw.at[plane, pl.ds(dst, inner)]))
        dst = pl.multiple_of(core * inner, 16)
        copies.append((halo, k_raw.at[plane, pl.ds(dst, outer)]))
    for plane, ref in ((core, e_own), (other, e_pair)):
        for chunk in range(sz.chunks):
            copies.append((
                ref.at[0, pl.ds(start, sz.e_rows), pl.ds(chunk * LANES, LANES)],
                e_raw.at[plane, pl.ds(chunk * sz.e_rows, sz.e_rows)],
            ))
    started = [pltpu.make_async_copy(a, b, sems.at[i]) for i, (a, b) in enumerate(copies)]
    for copy in started:
        copy.start()
    for copy in started:
        copy.wait()
    return first, start


def n_loads(sz):
    return 4 + 2 * sz.chunks


def load_scratch(sz):
    return [
        pltpu.VMEM((2, sz.ext * sz.per_row, LANES), BF16),
        pltpu.VMEM((2, sz.chunks * sz.e_rows, LANES), F32),
        pltpu.VMEM((2, sz.ext * sz.per_row, LANES), F32),
        pltpu.SemaphoreType.DMA((n_loads(sz),)),
    ]


def kappa_row(sz, k_wide, plane, row, point):
    return k_wide[plane, pl.ds(row * sz.per_row + point, sz.chunks, stride=sz.points), :]


def e_row(sz, e_raw, plane, row, first, start):
    at = jnp.clip(first + row - start, 0, sz.e_rows - 1)
    return e_raw[plane, pl.ds(at, sz.chunks, stride=sz.e_rows), :]


def inside(sz, row, first):
    if 2 <= row < 2 + sz.rows:
        return None
    at = first + row
    return jnp.where((at >= 0) & (at < sz.ny), 1.0, 0.0).astype(F32)


def masked(x, inside_row):
    return x if inside_row is None else x * inside_row


def along_z(chunks):
    lane = lax.broadcasted_iota(jnp.int32, (chunks, LANES), 1)
    sub = lax.broadcasted_iota(jnp.int32, (chunks, LANES), 0)
    last, front = lane == LANES - 1, lane == 0
    keep_down = jnp.where(sub == 0, 0.0, 1.0).astype(F32)
    keep_up = jnp.where(sub == chunks - 1, 0.0, 1.0).astype(F32)

    def both(x):
        before = jnp.where(last, pltpu.roll(x, 1, 0) * keep_down, x)
        after = jnp.where(front, pltpu.roll(x, chunks - 1, 0) * keep_up, x)
        return pltpu.roll(before, 1, 1) + pltpu.roll(after, LANES - 1, 1)

    return both


def edge_kernel(
    sz, k_own, k_pair, halo_own, halo_pair, e_own, e_pair, weight, low, high,
    first_msg, second_msg, scalars,
    k_raw, e_raw, k_wide, sems, message, out_sems,
):
    pair, _, _ = place()
    first, start = load_planes(
        sz, k_own, k_pair, halo_own, halo_pair, e_own, e_pair, k_raw, e_raw, sems
    )
    k_wide[...] = k_raw[...].astype(F32)
    both = along_z(sz.chunks)
    for at, ref in enumerate((weight, low, high)):
        scalars[at] = jnp.full((8, LANES), ref[0], F32)
    rows = range(1, sz.rows + 3)
    light = [
        {r: masked(e_row(sz, e_raw, i, r, first, start), inside(sz, r, first)) for r in rows}
        for i in range(2)
    ]
    step = 2 * sz.chunks
    for p in range(0, sz.points, 2):
        kappa, source, sums = {}, {}, {}
        for point in (p, p + 1):
            for i in range(2):
                for r in rows:
                    kappa[point, i, r] = kappa_row(sz, k_wide, i, r, point)
                    source[point, i, r] = kappa[point, i, r] * light[i][r]
        for point in (p, p + 1):
            for i in range(2):
                for r in range(2, 2 + sz.rows):
                    s = source[point, i, r]
                    near = source[point, i, r - 1] + source[point, i, r + 1] + both(s)
                    sums[point, i, r] = 2.0 * near - 12.0 * s + source[point, 1 - i, r]
        for i in range(2):
            for r in range(2, 2 + sz.rows):
                at = ((r - 2) * sz.points + p) * sz.chunks
                pairs = [kappa[q, i, r] for q in (p, p + 1)]
                message[i, at:at + step] = jnp.concatenate(pairs, axis=0).astype(BF16)
                pairs = [sums[q, i, r] for q in (p, p + 1)]
                at += sz.field
                message[i, at:at + step] = jnp.concatenate(pairs, axis=0).astype(BF16)
    for i in range(2):
        for r in range(0, sz.rows, 2):
            at = 2 * sz.field + r * sz.chunks
            pairs = [light[i][r + 2], light[i][r + 3]]
            message[i, at:at + step] = jnp.concatenate(pairs, axis=0).astype(BF16)
    odd = lax.rem(pair, 2)
    copies = [
        pltpu.make_async_copy(message.at[1 - odd], first_msg, out_sems.at[0]),
        pltpu.make_async_copy(message.at[odd], second_msg, out_sems.at[1]),
    ]
    for copy in copies:
        copy.start()
    for copy in copies:
        copy.wait()


def coefficients(weight, low, high):
    theta = (high + low) * 0.5
    delta = (high - low) * 0.5
    sigma = theta / delta
    rho0 = 1.0 / sigma
    rho1 = 1.0 / (2.0 * sigma - rho0)
    rho2 = 1.0 / (2.0 * sigma - rho1)
    a1, b1 = rho1 * rho0, 2.0 * rho1 / delta
    a2, b2 = rho2 * rho1, 2.0 * rho2 / delta
    c = a1 / theta + b1
    bt = b1 / theta
    c1 = (13.0 / 9.0) * (1.0 / theta + (1.0 + a2) * c + b2)
    mixed = (1.0 + a2) * bt + b2 / theta + b2 * c
    c2 = (-7.0 / 3.0) * mixed
    c3 = (313.0 / 81.0) * b2 * bt
    c4 = (-25.0 / 63.0) * mixed
    c5 = (115.0 / 189.0) * b2 * bt
    c7 = (53.0 / 441.0) * b2 * bt
    return weight, c1, c2, c3, c4, c5, c7


def inner_kernel(sz, k_own, k_pair, halo_own, halo_pair, e_own, e_pair, *refs):
    scalars = refs[:sz.n_quad]
    base, k_out, coeffs, k_raw, e_raw, k_wide, sems, by_point = refs[sz.n_quad:]
    pair, _, quad = place()
    first, start = load_planes(
        sz, k_own, k_pair, halo_own, halo_pair, e_own, e_pair, k_raw, e_raw, sems
    )
    k_wide[...] = k_raw[...].astype(F32)
    for k in range(sz.n_quad):
        by_point[lax.bitwise_xor(quad, k)] = scalars[k][...]
    both = along_z(sz.chunks)
    exists = (
        jnp.where(pair > 0, 1.0, 0.0).astype(F32),
        jnp.where(pair < sz.n_slab // 2 - 1, 1.0, 0.0).astype(F32),
    )
    rows = range(sz.ext)
    middle = range(1, sz.ext - 1)
    for p in range(sz.points):
        weight, c1, c2, c3, c4, c5, c7 = coefficients(*[by_point[p, i] for i in range(3)])
        coeffs[p, 0] = weight * c4
        coeffs[p, 1] = weight * c5
        coeffs[p, 2] = weight * c7
        kappa, source, lap, mix = {}, {}, {}, {}
        for i in range(2):
            for r in rows:
                light = masked(e_row(sz, e_raw, i, r, first, start), inside(sz, r, first))
                kappa[i, r] = kappa_row(sz, k_wide, i, r, p)
                source[i, r] = kappa[i, r] * light
        for i in range(2):
            for r in middle:
                s = source[i, r]
                near = source[i, r - 1] + source[i, r + 1] + both(s) + source[1 - i, r]
                lap[i, r] = masked(6.0 * s - near, inside(sz, r, first))
                mix[i, r] = c5 * kappa[i, r] * s + c7 * lap[i, r]
        for i in range(2):
            for r in range(2, 2 + sz.rows):
                s, k, m = source[i, r], kappa[i, r], mix[i, r]
                near = mix[i, r - 1] + mix[i, r + 1] + both(m) + mix[1 - i, r]
                inc = s * (c1 + k * (c2 + k * c3)) + lap[i, r] * (c4 + k * c5)
                inc = inc + 6.0 * m - near + exists[i] * c7 * s
                term = weight * (k * inc - s)
                if p == 0:
                    base[i, r - 2] = term
                else:
                    base[i, r - 2] += term
                k_out[i, (r - 2) * sz.points + p] = k


def join_kernel(
    sz, base, kappa, coeffs, first_msg, second_msg, own, far, near_buf, res, sems, out_sems
):
    pair, core, _ = place()
    odd = lax.rem(pair, 2)
    copies = [
        pltpu.make_async_copy(first_msg, near_buf.at[1 - odd], sems.at[0]),
        pltpu.make_async_copy(second_msg, near_buf.at[odd], sems.at[1]),
    ]
    for copy in copies:
        copy.start()
    for copy in copies:
        copy.wait()
    exists = (
        jnp.where(pair > 0, 1.0, 0.0).astype(F32),
        jnp.where(pair < sz.n_slab // 2 - 1, 1.0, 0.0).astype(F32),
    )
    step = 2 * sz.chunks
    for r in range(0, sz.rows, 2):
        lights = []
        for side in range(2):
            at = 2 * sz.field + r * sz.chunks
            wide = near_buf[side, at:at + step].astype(F32) * exists[side]
            lights.append((wide[:sz.chunks], wide[sz.chunks:]))
        for half in range(2):
            row = r + half
            total = [base[0, row], base[1, row]]
            for p in range(0, sz.points, 2):
                at = (row * sz.points + p) * sz.chunks
                wide_k = [near_buf[side, at:at + step].astype(F32) for side in range(2)]
                at += sz.field
                wide_u = [
                    near_buf[side, at:at + step].astype(F32) * exists[side] for side in range(2)
                ]
                for q in range(2):
                    cut = slice(q * sz.chunks, (q + 1) * sz.chunks)
                    w4, w5, w7 = [coeffs[p + q, i] for i in range(3)]
                    near_s = [wide_k[side][cut] * lights[side][half] for side in range(2)]
                    for i in range(2):
                        k = kappa[i, row * sz.points + p + q]
                        inc = w7 * (wide_u[i][cut] + near_s[1 - i])
                        inc = inc - near_s[i] * (w4 + w5 * (k + wide_k[i][cut]))
                        total[i] = total[i] + k * inc
            for i in range(2):
                res[i, row * sz.chunks:(row + 1) * sz.chunks] = total[i]
    copies = [
        pltpu.make_async_copy(res.at[core], own, out_sems.at[0]),
        pltpu.make_async_copy(res.at[1 - core], far, out_sems.at[1]),
    ]
    for copy in copies:
        copy.start()
    for copy in copies:
        copy.wait()


def pick_kernel(sz, most, counts, *refs):
    pieces = refs[:sz.n_quad]
    out, rows, sems = refs[sz.n_quad:]
    _, _, quad = place()
    block = 2 * sz.plain
    copies = []
    for k in range(sz.n_quad):
        at = pl.multiple_of(lax.bitwise_xor(quad, k) * block, 8)
        copies.append(pltpu.make_async_copy(pieces[k], rows.at[pl.ds(at, block)], sems.at[k]))
    for copy in copies:
        copy.start()
    offset, count = jnp.int32(0), jnp.int32(0)
    for r in range(sz.n_quad):
        offset = offset + jnp.where(r < quad, counts[0, r], 0)
        count = count + jnp.where(r == quad, counts[0, r], 0)
    for copy in copies:
        copy.wait()
    sub = lax.broadcasted_iota(jnp.int32, (8, LANES), 0)
    for i in range(0, most, 8):
        got = rows[pl.ds(offset + i, 8), :]
        out[i:i + 8] = jnp.where(sub + i < count, got, 0.0)


def exchanges(n_slab, n_quad):
    pairs = n_slab // 2

    def listed(move):
        moved = []
        for pair in range(pairs):
            for core in range(2):
                for quad in range(n_quad):
                    a, b, c = move(pair, core, quad)
                    moved.append(((pair * 2 + core) * n_quad + quad, (a * 2 + b) * n_quad + c))
        return moved

    def along(parity):
        def move(pair, core, quad):
            to = pair + 1 if pair % 2 == parity else pair - 1
            if 0 <= to < pairs:
                return to, core, quad
            return pair, 1 - core, quad

        return listed(move)

    return {
        "swap": listed(lambda a, b, c: (a, 1 - b, c)),
        "own": listed(lambda a, b, c: (a, b, (c + 1 - 2 * b) % n_quad)),
        "pair": listed(lambda a, b, c: (a, 1 - b, (c - 1 + 2 * b) % n_quad)),
        "first": along(0),
        "second": along(1),
        "quad": [listed(lambda a, b, c, k=k: (a, b, c ^ k)) for k in range(1, n_quad)],
    }


def shape(*dims, dtype=F32):
    return jax.ShapeDtypeStruct(dims, dtype)


def per_device(absorption, emission, weights, low_bound, high_bound, row_counts):
    n_slab, n_quad = lax.axis_size("slab"), lax.axis_size("quad")
    sz = Sizes(absorption, emission, n_slab, n_quad)
    to = exchanges(n_slab, n_quad)

    def send(x, pairs):
        return lax.ppermute(x, ("slab", "quad"), pairs)

    core = lax.axis_index("slab") % 2
    k_own = absorption.reshape(sz.points, -1, LANES).transpose(1, 0, 2).reshape(-1, LANES)
    edge = 2 * sz.per_row
    head, tail = k_own[:edge], k_own[-edge:]
    halo_own = send(jnp.where(core == 0, tail, head), to["own"])
    halo_pair = send(jnp.where(core == 0, head, tail), to["pair"])
    k_pair = send(k_own, to["swap"])
    e_pair = send(emission, to["swap"])

    params = pltpu.CompilerParams(vmem_limit_bytes=32 * 1024 * 1024)
    length = 2 * sz.field + sz.plain
    first_msg, second_msg, scalars = pl.pallas_call(
        functools.partial(edge_kernel, sz),
        name="edge_planes",
        out_shape=(
            shape(length, LANES, dtype=BF16),
            shape(length, LANES, dtype=BF16),
            shape(3, 8, LANES),
        ),
        in_specs=[ANY] * 6 + [SMEM] * 3,
        out_specs=(ANY, ANY, VMEM),
        scratch_shapes=load_scratch(sz) + [
            pltpu.VMEM((2, length, LANES), BF16),
            pltpu.SemaphoreType.DMA((2,)),
        ],
        compiler_params=params,
        cost_estimate=pl.CostEstimate(flops=8_000_000, bytes_accessed=2_000_000, transcendentals=0),
    )(k_own, k_pair, halo_own, halo_pair, emission, e_pair, weights, low_bound, high_bound)

    near_first = send(first_msg, to["first"])
    near_second = send(second_msg, to["second"])
    all_scalars = [scalars] + [send(scalars, pairs) for pairs in to["quad"]]

    base, kappa, coeffs = pl.pallas_call(
        functools.partial(inner_kernel, sz),
        name="inner_planes",
        out_shape=(
            shape(2, sz.rows, sz.chunks, LANES),
            shape(2, sz.rows * sz.points, sz.chunks, LANES),
            shape(sz.points, 3, 8, LANES),
        ),
        in_specs=[ANY] * 6 + [VMEM] * n_quad,
        out_specs=(VMEM, VMEM, VMEM),
        scratch_shapes=load_scratch(sz) + [pltpu.VMEM((n_quad, 3, 8, LANES), F32)],
        compiler_params=params,
        cost_estimate=pl.CostEstimate(flops=16_000_000, bytes_accessed=3_000_000, transcendentals=0),
    )(k_own, k_pair, halo_own, halo_pair, emission, e_pair, *all_scalars)

    own, far = pl.pallas_call(
        functools.partial(join_kernel, sz),
        name="join_planes",
        out_shape=(shape(sz.plain, LANES), shape(sz.plain, LANES)),
        in_specs=[VMEM, VMEM, VMEM, ANY, ANY],
        out_specs=(ANY, ANY),
        scratch_shapes=[
            pltpu.VMEM((2, length, LANES), BF16),
            pltpu.VMEM((2, sz.plain, LANES), F32),
            pltpu.SemaphoreType.DMA((2,)),
            pltpu.SemaphoreType.DMA((2,)),
        ],
        compiler_params=params,
        cost_estimate=pl.CostEstimate(flops=4_000_000, bytes_accessed=2_000_000, transcendentals=0),
    )(base, kappa, coeffs, near_first, near_second)

    back = send(far, to["swap"])
    lower = jnp.where(core == 0, own, back)
    upper = jnp.where(core == 0, back, own)
    rows = jnp.concatenate([lower, upper], axis=0)
    pieces = [rows] + [send(rows, pairs) for pairs in to["quad"]]

    total_rows = n_quad * 2 * sz.plain
    most = 2 * total_rows // n_quad
    return pl.pallas_call(
        functools.partial(pick_kernel, sz, most),
        name="pick_rows",
        out_shape=shape(most, LANES),
        in_specs=[SMEM] + [ANY] * n_quad,
        out_specs=VMEM,
        scratch_shapes=[
            pltpu.VMEM((total_rows + most, LANES), F32),
            pltpu.SemaphoreType.DMA((n_quad,)),
        ],
        compiler_params=params,
        cost_estimate=pl.CostEstimate(flops=200_000, bytes_accessed=1_000_000, transcendentals=0),
    )(row_counts, *pieces)


def solution(mesh):
    in_specs = (
        P(None, ("slab", "quad")),
        P("slab", None, None),
        P("quad"),
        P("quad"),
        P("quad"),
        P("slab", None),
    )
    out_specs = P(("slab", "quad"), None)
    return jax.shard_map(
        per_device, mesh=mesh, in_specs=in_specs, out_specs=out_specs, check_vma=False
    )
```

```python
import functools

import jax
import jax.numpy as jnp
from jax import lax
from jax.experimental import pallas as pl
from jax.experimental.pallas import tpu as pltpu
from jax.sharding import PartitionSpec as P

LANES = 128
F32 = jnp.float32
BF16 = jnp.bfloat16
HEADROOM = 14.5
SOURCE, LAPLACE = 7.0 / 3.0, 25.0 / 63.0
CUBE, CROSS, TWICE = 313.0 / 81.0, 115.0 / 189.0, 53.0 / 441.0
ANY = pl.BlockSpec(memory_space=pl.ANY)
SMEM = pl.BlockSpec(memory_space=pltpu.SMEM)
VMEM = pl.BlockSpec(memory_space=pltpu.VMEM)


class Sizes:
    def __init__(self, absorption, emission, n_slab, n_quad):
        self.points = absorption.shape[0]
        self.ny, self.nz = emission.shape[1:]
        self.chunks = self.nz // LANES
        self.rows_quad = absorption.shape[1] // self.nz
        self.rows = self.rows_quad // 2
        self.ext = self.rows + 4
        self.per_row = self.points * self.chunks
        self.e_rows = min(self.ny, (6 + self.ext + 7) // 8 * 8)
        self.n_slab, self.n_quad = n_slab, n_quad
        self.field = self.rows * self.per_row
        self.plain = self.rows * self.chunks


def place():
    slab = lax.axis_index("slab")
    return lax.div(slab, 2), lax.rem(slab, 2), lax.axis_index("quad")


def part_of(sz):
    _, core, quad = place()
    first = quad * sz.rows_quad + core * sz.rows - 2
    start = jnp.clip(lax.div(first + 8, 8) * 8 - 8, 0, sz.ny - sz.e_rows)
    return first, pl.multiple_of(start, 8)


def part_copies(sz, k_plane, e_plane, k_part, e_part):
    _, core, _ = place()
    _, start = part_of(sz)
    src = pl.multiple_of(core * ((sz.rows - 2) * sz.per_row), 16)
    copies = [(k_plane.at[pl.ds(src, (sz.rows + 2) * sz.per_row)], k_part)]
    for chunk in range(sz.chunks):
        copies.append((
            e_plane.at[0, pl.ds(start, sz.e_rows), pl.ds(chunk * LANES, LANES)],
            e_part.at[pl.ds(chunk * sz.e_rows, sz.e_rows)],
        ))
    return copies


def run_copies(copies, sems):
    started = [pltpu.make_async_copy(a, b, sems.at[i]) for i, (a, b) in enumerate(copies)]
    for copy in started:
        copy.start()
    for copy in started:
        copy.wait()


def part_kernel(sz, k_own, e_own, k_part, e_part, sems):
    run_copies(part_copies(sz, k_own, e_own, k_part, e_part), sems)


def load_planes(sz, k_part, e_part, k_pair, e_pair, k_raw, e_raw, sems):
    _, core, _ = place()
    other = 1 - core
    inner = (sz.rows + 2) * sz.per_row
    outer = 2 * sz.per_row
    at = pl.ds(pl.multiple_of(other * outer, 16), inner)
    copies = part_copies(sz, k_pair, e_pair, k_raw.at[other, at], e_raw.at[other])
    copies.append((k_part, k_raw.at[core, at]))
    copies.append((e_part, e_raw.at[core]))
    run_copies(copies, sems)
    return part_of(sz)


def n_loads(sz):
    return 3 + sz.chunks


def load_scratch(sz):
    return [
        pltpu.VMEM((2, sz.ext * sz.per_row, LANES), BF16),
        pltpu.VMEM((2, sz.chunks * sz.e_rows, LANES), F32),
        pltpu.VMEM((2, sz.ext * sz.per_row, LANES), F32),
        pltpu.SemaphoreType.DMA((n_loads(sz),)),
    ]


def kappa_row(sz, k_wide, plane, row, point):
    return k_wide[plane, pl.ds(row * sz.per_row + point, sz.chunks, stride=sz.points), :]


def e_row(sz, e_raw, plane, row, first, start):
    at = jnp.clip(first + row - start, 0, sz.e_rows - 1)
    return e_raw[plane, pl.ds(at, sz.chunks, stride=sz.e_rows), :]


def inside(sz, row, first):
    if 2 <= row < 2 + sz.rows:
        return None
    at = first + row
    return jnp.where((at >= 0) & (at < sz.ny), 1.0, 0.0).astype(F32)


def masked(x, inside_row):
    return x if inside_row is None else x * inside_row


def along_z(chunks):
    lane = lax.broadcasted_iota(jnp.int32, (chunks, LANES), 1)
    sub = lax.broadcasted_iota(jnp.int32, (chunks, LANES), 0)
    last, front = lane == LANES - 1, lane == 0
    keep_down = jnp.where(sub == 0, 0.0, 1.0).astype(F32)
    keep_up = jnp.where(sub == chunks - 1, 0.0, 1.0).astype(F32)

    def both(x):
        before = jnp.where(last, pltpu.roll(x, 1, 0) * keep_down, x)
        after = jnp.where(front, pltpu.roll(x, chunks - 1, 0) * keep_up, x)
        return pltpu.roll(before, 1, 1) + pltpu.roll(after, LANES - 1, 1)

    return both


def edge_kernel(
    sz, k_part, e_part, k_pair, e_pair, first_msg, second_msg, e_edge, fields,
    k_raw, e_raw, k_wide, sems, message, out_sems,
):
    pair, core, _ = place()
    first, start = load_planes(sz, k_part, e_part, k_pair, e_pair, k_raw, e_raw, sems)
    k_wide[...] = k_raw[...].astype(F32)
    both = along_z(sz.chunks)
    rows = range(1, sz.rows + 3)
    last = sz.rows + 1
    light = [{r: e_row(sz, e_raw, i, r, first, start) for r in rows} for i in range(2)]
    for i in range(2):
        for slot, r in enumerate((0, 1, last + 1, last + 2)):
            e_edge[i, slot] = masked(e_row(sz, e_raw, i, r, first, start), inside(sz, r, first))
    step = 2 * sz.chunks
    for p in range(0, sz.points, 2):
        kappa, source, sums = {}, {}, {}
        for point in (p, p + 1):
            for i in range(2):
                for r in rows:
                    kappa[point, i, r] = kappa_row(sz, k_wide, i, r, point)
                    s = kappa[point, i, r] * light[i][r]
                    if r == 1:
                        s = jnp.where(core == 1, s, 0.0)
                    if r == last + 1:
                        s = jnp.where(core == 0, s, 0.0)
                    source[point, i, r] = s
        for point in (p, p + 1):
            for i in range(2):
                for r in range(2, 2 + sz.rows):
                    s, k, other = source[point, i, r], kappa[point, i, r], source[point, 1 - i, r]
                    near = source[point, i, r - 1] + source[point, i, r + 1] + both(s)
                    lap = 6.0 * s - near - other
                    at = (r - 2) * sz.points + point
                    fields[0, i, at] = k
                    fields[1, i, at] = s
                    fields[2, i, at] = lap
                    sums[point, i, r] = -TWICE * (2.0 * lap + other)
        for i in range(2):
            for r in range(2, 2 + sz.rows):
                at = ((r - 2) * sz.points + p) * sz.chunks
                pairs = [sums[q, i, r] for q in (p, p + 1)]
                message[i, at:at + step] = jnp.concatenate(pairs, axis=0).astype(BF16)
    odd = lax.rem(pair, 2)
    copies = [
        pltpu.make_async_copy(message.at[1 - odd], first_msg, out_sems.at[0]),
        pltpu.make_async_copy(message.at[odd], second_msg, out_sems.at[1]),
    ]
    for copy in copies:
        copy.start()
    for copy in copies:
        copy.wait()


def beyond_kernel(
    sz, first_in, second_in, halo, e_edge, parts, first_msg, second_msg, two_points,
    k_wide, edge_rows, in_sems, out_sems,
):
    del first_in, second_in
    pair, core, _ = place()
    odd = lax.rem(pair, 2)
    at = pl.multiple_of(core * ((sz.rows - 1) * sz.per_row), 16)
    places = [ref.at[pl.ds(at, sz.per_row)] for ref in (first_msg, second_msg)]
    copies = [pltpu.make_async_copy(places[m], edge_rows.at[m], in_sems.at[m]) for m in range(2)]
    for copy in copies:
        copy.start()
    two_points[:16] = parts[...]
    two_points[16:] = halo[4 * sz.per_row:]
    for plane in range(2):
        k_wide[plane] = halo[plane * 2 * sz.per_row:(plane + 1) * 2 * sz.per_row].astype(F32)
    for copy in copies:
        copy.wait()
    step = 2 * sz.chunks
    for m, plane in enumerate((1 - odd, odd)):
        light = (2.0 * TWICE) * e_edge[plane, 1 + core]
        for p in range(0, sz.points, 2):
            pairs = [
                light * k_wide[plane, pl.ds((1 - core) * sz.per_row + q, sz.chunks, stride=sz.points), :]
                for q in (p, p + 1)
            ]
            cut = slice(p * sz.chunks, p * sz.chunks + step)
            wide = edge_rows[m, cut].astype(F32) + jnp.concatenate(pairs, axis=0)
            edge_rows[m, cut] = wide.astype(BF16)
    copies = [pltpu.make_async_copy(edge_rows.at[m], places[m], out_sems.at[m]) for m in range(2)]
    for copy in copies:
        copy.start()
    for copy in copies:
        copy.wait()


def coefficients(weight, low, high):
    theta = (high + low) * 0.5
    delta = (high - low) * 0.5
    sigma = theta / delta
    rho0 = 1.0 / sigma
    rho1 = 1.0 / (2.0 * sigma - rho0)
    rho2 = 1.0 / (2.0 * sigma - rho1)
    a1, b1 = rho1 * rho0, 2.0 * rho1 / delta
    a2, b2 = rho2 * rho1, 2.0 * rho2 / delta
    c = a1 / theta + b1
    bt = b1 / theta
    c1 = (13.0 / 9.0) * (1.0 / theta + (1.0 + a2) * c + b2)
    mixed = (1.0 + a2) * bt + b2 / theta + b2 * c
    return weight, c1, mixed, b2 * bt


def inner_kernel(
    sz, fields, e_edge, k_part, k_pair, halo, first_k, second_k, sums,
    k_raw, k_wide, near_k, near_wide, sems,
):
    pair, core, quad = place()
    odd = lax.rem(pair, 2)
    other = 1 - core
    two = 2 * sz.per_row
    outer = pl.ds(pl.multiple_of(core * two, 16), two)
    inner = pl.ds(pl.multiple_of(other * two, 16), two)
    from_part = pl.ds(pl.multiple_of(other * sz.field, 16), two)
    from_pair = pl.multiple_of(core * (sz.field - two) + other * sz.field, 16)
    run_copies(
        [
            (first_k, near_k.at[1 - odd]),
            (second_k, near_k.at[odd]),
            (halo.at[pl.ds(0, two)], k_raw.at[0, outer]),
            (halo.at[pl.ds(two, two)], k_raw.at[1, outer]),
            (k_part.at[from_part], k_raw.at[core, inner]),
            (k_pair.at[pl.ds(from_pair, two)], k_raw.at[other, inner]),
        ],
        sems,
    )
    k_wide[...] = k_raw[...].astype(F32)
    near_wide[...] = near_k[...].astype(F32)
    both = along_z(sz.chunks)
    exists = (
        jnp.where(pair > 0, 1.0, 0.0).astype(F32),
        jnp.where(pair < sz.n_slab // 2 - 1, 1.0, 0.0).astype(F32),
    )
    for side in range(2):
        near_wide[side, sz.field:] = near_wide[side, sz.field:] * exists[side]
    last = sz.rows + 1
    slots = {0: 0, 1: 1, last + 1: 2, last + 2: 3}
    own = range(2, last + 1)
    for p in range(sz.points):
        kappa, source, lap, mix = {}, {}, {}, {}
        for i in range(2):
            for r, slot in slots.items():
                kappa[i, r] = kappa_row(sz, k_wide, i, slot, p)
                source[i, r] = kappa[i, r] * e_edge[i, slot]
            for r in own:
                at = (r - 2) * sz.points + p
                kappa[i, r], source[i, r], lap[i, r] = [fields[f, i, at] for f in range(3)]
            lap[i, 2] = lap[i, 2] - jnp.where(core == 0, source[i, 1], 0.0)
            lap[i, last] = lap[i, last] - jnp.where(core == 1, source[i, last + 1], 0.0)
        first = quad * sz.rows_quad + core * sz.rows - 2
        for i in range(2):
            for r in (1, last + 1):
                s = source[i, r]
                near = source[i, r - 1] + source[i, r + 1] + both(s) + source[1 - i, r]
                lap[i, r] = masked(6.0 * s - near, inside(sz, r, first))
            for r in range(1, last + 2):
                mix[i, r] = CROSS * (kappa[i, r] * source[i, r]) + TWICE * lap[i, r]
        for i in range(2):
            for r in own:
                s, k, m = source[i, r], kappa[i, r], mix[i, r]
                near = mix[i, r - 1] + mix[i, r + 1] + both(m) + mix[1 - i, r]
                near_at = [kappa_row(sz, near_wide, side, r - 2, p) for side in range(2)]
                near_s = [
                    near_at[side]
                    * near_wide[side, pl.ds(sz.field + r - 2, sz.chunks, stride=sz.rows), :]
                    for side in range(2)
                ]
                d = lap[i, r] - near_s[i]
                at = (r - 2) * sz.points + p
                sums[0, i, at] = SOURCE * (k * s) + LAPLACE * d
                sums[1, i, at] = (
                    k * (CUBE * (k * s) + CROSS * d)
                    + (6.0 * m - near)
                    - CROSS * (near_at[i] * near_s[i])
                    + TWICE * (exists[i] * s + near_s[1 - i])
                )


def join_kernel(sz, fields, sums, first_msg, second_msg, *refs):
    scalars, (own, far, by_point, res, coded, out_sems) = refs[:-6], refs[-6:]
    pair, core, quad = place()
    odd = lax.rem(pair, 2)
    if sz.n_quad == 4:
        side = 2 * core - 1
        for ref, at in zip(scalars, (quad, quad + 2)):
            wide = ref[...].astype(F32)
            for half in range(2):
                point = lax.rem(at + half * side + 4, 4)
                for i in range(3):
                    row = 16 * half + i
                    x = (wide[row:row + 1] + wide[row + 3:row + 4]) + wide[row + 6:row + 7]
                    by_point[point, i] = jnp.broadcast_to(x, (8, LANES))
    else:
        k = 0
        for ref in scalars:
            for i in range(ref.shape[0]):
                by_point[lax.bitwise_xor(quad, k)] = ref[i]
                k += 1
    exists = (
        jnp.where(pair > 0, 1.0, 0.0).astype(F32),
        jnp.where(pair < sz.n_slab // 2 - 1, 1.0, 0.0).astype(F32),
    )
    step = 2 * sz.chunks
    for p in range(0, sz.points, 2):
        known = [coefficients(*[by_point[p + q, i] for i in range(3)]) for q in range(2)]
        for msg, plane in ((first_msg, 1 - odd), (second_msg, odd)):
            there = jnp.where(plane == 0, exists[0], exists[1])
            for row in range(sz.rows):
                at = (row * sz.points + p) * sz.chunks
                wide = msg[at:at + step].astype(F32) * there
                total = 0.0
                for q in range(2):
                    weight, c1, mixed, beta = known[q]
                    at = row * sz.points + p + q
                    k, s = fields[0, plane, at], fields[1, plane, at]
                    twice = sums[1, plane, at] + wide[q * sz.chunks:(q + 1) * sz.chunks]
                    inc = c1 * s - mixed * sums[0, plane, at] + beta * twice
                    total = total + weight * (k * inc - s)
                if p == 0:
                    res[plane, row] = total
                else:
                    res[plane, row] += total
    for i in range(2):
        top = jnp.abs(res[i, 0])
        for row in range(1, sz.rows):
            top = jnp.maximum(top, jnp.abs(res[i, row]))
        power = jnp.ceil(jnp.log2(jnp.maximum(top, 1e-30)))
        scale = jnp.exp2(HEADROOM - power)
        for row in range(0, sz.rows, 2):
            pairs = [jnp.floor(res[i, row + h] * scale + 0.5) for h in range(2)]
            pairs = jnp.concatenate(pairs, axis=0).astype(jnp.int32).astype(jnp.int16)
            coded[i, row * sz.chunks:row * sz.chunks + step] = pairs
        pairs = jnp.concatenate([power, power], axis=0).astype(jnp.int32).astype(jnp.int16)
        coded[i, sz.plain:sz.plain + step] = pairs
    copies = [
        pltpu.make_async_copy(coded.at[core], own, out_sems.at[0]),
        pltpu.make_async_copy(coded.at[1 - core], far, out_sems.at[1]),
    ]
    for copy in copies:
        copy.start()
    for copy in copies:
        copy.wait()


def pick_kernel(sz, most, counts, *refs):
    pieces = refs[:sz.n_quad]
    out, rows = refs[sz.n_quad:]
    _, _, quad = place()
    step = 2 * sz.chunks
    coded = sz.plain + step
    for k in range(sz.n_quad):
        start = lax.bitwise_xor(quad, k) * (2 * sz.plain)
        for half in range(2):
            at = half * coded
            power = pieces[k][at + sz.plain:at + coded].astype(jnp.int32).astype(F32)
            scale = jnp.exp2(power - HEADROOM)
            for r in range(0, sz.plain, step):
                wide = pieces[k][at + r:at + r + step].astype(jnp.int32).astype(F32) * scale
                to = pl.multiple_of(start + half * sz.plain + r, step)
                rows[pl.ds(to, step)] = wide
    offset, count = jnp.int32(0), jnp.int32(0)
    for r in range(sz.n_quad):
        offset = offset + jnp.where(r < quad, counts[0, r], 0)
        count = count + jnp.where(r == quad, counts[0, r], 0)
    sub = lax.broadcasted_iota(jnp.int32, (8, LANES), 0)
    for i in range(0, most, 8):
        got = rows[pl.ds(offset + i, 8), :]
        out[i:i + 8] = jnp.where(sub + i < count, got, 0.0)


def exchanges(n_slab, n_quad):
    pairs = n_slab // 2

    def listed(move):
        moved = []
        for pair in range(pairs):
            for core in range(2):
                for quad in range(n_quad):
                    a, b, c = move(pair, core, quad)
                    moved.append(((pair * 2 + core) * n_quad + quad, (a * 2 + b) * n_quad + c))
        return moved

    def along(parity):
        def move(pair, core, quad):
            to = pair + 1 if pair % 2 == parity else pair - 1
            if 0 <= to < pairs:
                return to, core, quad
            return pair, 1 - core, quad

        return listed(move)

    return {
        "swap": listed(lambda a, b, c: (a, 1 - b, c)),
        "beside": listed(lambda a, b, c: (a, 1 - b, (c - 1 + 2 * b) % n_quad)),
        "first": along(0),
        "second": along(1),
        "quad": [listed(lambda a, b, c, k=k: (a, b, c ^ k)) for k in range(1, n_quad)],
    }


def in_parts(x):
    parts = []
    for _ in range(2):
        parts.append(lax.reduce_precision(x, 8, 7))
        x = x - parts[-1]
    rows = jnp.concatenate(parts + [x]).astype(BF16)
    return jnp.concatenate([rows, jnp.zeros((16 - rows.shape[0], LANES), BF16)])


def shape(*dims, dtype=F32):
    return jax.ShapeDtypeStruct(dims, dtype)


def per_device(absorption, emission, weights, low_bound, high_bound, row_counts):
    n_slab, n_quad = lax.axis_size("slab"), lax.axis_size("quad")
    sz = Sizes(absorption, emission, n_slab, n_quad)
    to = exchanges(n_slab, n_quad)

    def send(x, pairs):
        return lax.ppermute(x, ("slab", "quad"), pairs)

    params = pltpu.CompilerParams(vmem_limit_bytes=24 * 1024 * 1024)

    def kernel(body, **kwargs):
        return pl.pallas_call(functools.partial(body, sz), compiler_params=params, **kwargs)

    def cost(flops, bytes_accessed):
        return pl.CostEstimate(flops=flops // 1000000, bytes_accessed=bytes_accessed // 100000, transcendentals=0)

    core = lax.axis_index("slab") % 2
    odd = lax.axis_index("slab") // 2 % 2
    k_own = absorption.reshape(sz.points, -1, LANES).transpose(1, 0, 2).reshape(-1, LANES)
    k_pair = send(k_own, to["swap"])
    e_pair = send(emission, to["swap"])

    edge = 2 * sz.per_row
    k_part, e_part = kernel(
        part_kernel,
        name="own_part",
        out_shape=(
            shape(sz.field + edge, LANES, dtype=BF16),
            shape(sz.chunks * sz.e_rows, LANES),
        ),
        in_specs=[ANY] * 2,
        out_specs=(ANY, ANY),
        scratch_shapes=[pltpu.SemaphoreType.DMA((1 + sz.chunks,))],
        cost_estimate=cost(0, 600_000),
    )(
        pltpu.with_memory_space_constraint(k_own, pltpu.HBM),
        pltpu.with_memory_space_constraint(emission, pltpu.HBM),
    )

    def cut(x, at, size):
        return lax.dynamic_slice_in_dim(x, core * at, size, 0)

    own_edge = cut(k_part, sz.field, edge)
    pair_edge = cut(k_pair, 2 * sz.field - edge, edge)
    lower, upper = jnp.where(core == 0, own_edge, pair_edge), jnp.where(core == 0, pair_edge, own_edge)
    own_scalars = (weights, low_bound, high_bound)
    scalars = jnp.stack([jnp.broadcast_to(x, (8, LANES)) for x in own_scalars])[None]
    halo = jnp.concatenate([lower, upper])
    if n_quad == 4:
        parts = in_parts(scalars[0, :, 0])
        halo = send(jnp.concatenate([halo, parts]), to["beside"])
    else:
        parts = jnp.zeros((16, LANES), BF16)
        halo = send(jnp.concatenate([halo, parts]), to["beside"])
        scalars = [scalars]
        for bit in range(n_quad.bit_length() - 1):
            scalars = [jnp.concatenate(scalars)]
            scalars.append(send(scalars[0], to["quad"][(1 << bit) - 1]))

    first_row = lax.axis_index("quad") * sz.rows_quad + core * sz.rows
    kept = jnp.clip((first_row + 6) // 8 * 8 - 8, 0, sz.ny - sz.e_rows)
    own_e = lax.dynamic_slice_in_dim(
        e_part.reshape(sz.chunks, sz.e_rows, LANES), first_row - kept, sz.rows, 1
    )
    pair_e = lax.dynamic_slice_in_dim(e_pair[0], first_row, sz.rows, 0)
    pair_e = pair_e.reshape(sz.rows, sz.chunks, LANES).transpose(1, 0, 2)
    own_half, pair_half = [
        jnp.concatenate([k, e.astype(BF16).reshape(sz.plain, LANES)])
        for k, e in ((cut(k_part, edge, sz.field), own_e), (cut(k_pair, sz.field, sz.field), pair_e))
    ]
    own_first = core == 1 - odd
    k_first = send(jnp.where(own_first, own_half, pair_half), to["first"])
    k_second = send(jnp.where(own_first, pair_half, own_half), to["second"])

    length = sz.field
    first_msg, second_msg, e_edge, fields = kernel(
        edge_kernel,
        name="edge_planes",
        out_shape=(
            shape(length, LANES, dtype=BF16),
            shape(length, LANES, dtype=BF16),
            shape(2, 4, sz.chunks, LANES),
            shape(3, 2, sz.rows * sz.points, sz.chunks, LANES),
        ),
        in_specs=[ANY] * 4,
        out_specs=(ANY, ANY, VMEM, VMEM),
        scratch_shapes=load_scratch(sz) + [
            pltpu.VMEM((2, length, LANES), BF16),
            pltpu.SemaphoreType.DMA((2,)),
        ],
        cost_estimate=cost(8_000_000, 2_000_000),
    )(k_part, e_part, k_pair, e_pair)

    first_msg, second_msg, two_points = kernel(
        beyond_kernel,
        name="beyond_rows",
        out_shape=(
            shape(length, LANES, dtype=BF16),
            shape(length, LANES, dtype=BF16),
            shape(32, LANES, dtype=BF16),
        ),
        in_specs=[ANY, ANY, VMEM, VMEM, VMEM],
        out_specs=(ANY, ANY, VMEM),
        scratch_shapes=[
            pltpu.VMEM((2, edge, LANES), F32),
            pltpu.VMEM((2, sz.per_row, LANES), BF16),
            pltpu.SemaphoreType.DMA((2,)),
            pltpu.SemaphoreType.DMA((2,)),
        ],
        input_output_aliases={0: 0, 1: 1},
        cost_estimate=cost(100_000, 100_000),
    )(first_msg, second_msg, halo, e_edge, parts)

    near_first = send(first_msg, to["first"])
    near_second = send(second_msg, to["second"])

    sums = kernel(
        inner_kernel,
        name="inner_planes",
        out_shape=shape(2, 2, sz.rows * sz.points, sz.chunks, LANES),
        in_specs=[VMEM] * 2 + [ANY] * 5,
        out_specs=VMEM,
        scratch_shapes=[
            pltpu.VMEM((2, 4 * sz.per_row, LANES), BF16),
            pltpu.VMEM((2, 4 * sz.per_row, LANES), F32),
            pltpu.VMEM((2, sz.field + sz.plain, LANES), BF16),
            pltpu.VMEM((2, sz.field + sz.plain, LANES), F32),
            pltpu.SemaphoreType.DMA((6,)),
        ],
        cost_estimate=cost(16_000_000, 3_000_000),
    )(fields, e_edge, k_part, k_pair, halo, k_first, k_second)
    if n_quad == 4:
        opposite = [(i, i // n_quad * n_quad + (i + 2) % n_quad) for i in range(n_slab * n_quad)]
        two_on = send(two_points, opposite)
        scalars = [two_points, two_on]

    coded = sz.plain + 2 * sz.chunks
    own, far = kernel(
        join_kernel,
        name="join_planes",
        out_shape=(shape(coded, LANES, dtype=jnp.int16), shape(coded, LANES, dtype=jnp.int16)),
        in_specs=[VMEM] * (4 + len(scalars)),
        out_specs=(ANY, ANY),
        scratch_shapes=[
            pltpu.VMEM((n_quad, 3, 8, LANES), F32),
            pltpu.VMEM((2, sz.rows, sz.chunks, LANES), F32),
            pltpu.VMEM((2, coded, LANES), jnp.int16),
            pltpu.SemaphoreType.DMA((2,)),
        ],
        cost_estimate=cost(4_000_000, 2_000_000),
    )(fields, sums, near_first, near_second, *scalars)

    back = send(far, to["swap"])
    lower = jnp.where(core == 0, own, back)
    upper = jnp.where(core == 0, back, own)
    rows = jnp.concatenate([lower, upper], axis=0)
    pieces = [rows] + [send(rows, pairs) for pairs in to["quad"]]

    total_rows = n_quad * 2 * sz.plain
    most = 2 * total_rows // n_quad
    return pl.pallas_call(
        functools.partial(pick_kernel, sz, most),
        name="pick_rows",
        out_shape=shape(most, LANES),
        in_specs=[SMEM] + [VMEM] * n_quad,
        out_specs=VMEM,
        scratch_shapes=[pltpu.VMEM((total_rows + most, LANES), F32)],
        compiler_params=params,
        cost_estimate=cost(200_000, 1_000_000),
    )(row_counts, *pieces)


def solution(mesh):
    in_specs = (
        P(None, ("slab", "quad")),
        P("slab", None, None),
        P("quad"),
        P("quad"),
        P("quad"),
        P("slab", None),
    )
    out_specs = P(("slab", "quad"), None)
    return jax.shard_map(
        per_device, mesh=mesh, in_specs=in_specs, out_specs=out_specs, check_vma=False
    )
```
